256 devices in a mesh: bins: 64 (over x, z, core), panel: 4 (over y).
Axes of the slice: x: 4, y: 4, z: 8, core: 2. Of those that a mesh axis runs over, the one named last changes fastest.
Arguments:
- records: bfloat16 [16, 4096, 9216], P('panel', 'bins'), may hold values from -6 to 6
- valid: int32 [16, 4096], P('panel', 'bins'), may hold values 0 or 1
- offsets: int32 [16, 16], replicated, may hold values from 0 to 8192, as said below
Outputs:
- csd: bfloat16 [64, 4096, 4096], P('bins', 'panel')
The draws below stay inside these ranges and needn't reach their ends.
Inputs may be any that keep to these rules, and one draw needn't show every extreme that they name: offsets[w, s] lies between s * 512 and (s + 1) * 512.
All inputs are finite; a program needn't handle non-finite values. No bound on the sum of `valid` on one device may be relied on, other than what follows from the above.
Results may differ from the reference program's by a relative error of at most 0.007.
Values may be sent and summed in bfloat16 or wider, within the bound.
A program may use at most 64 MiB of HBM per device.

```python
import jax
import jax.numpy as jnp
from jax import lax

C = 4096
SEGLEN = 1024
HOP = 512
SEG = 16
BAND0 = 64
F = 64
WIN = 16
REC = 9216


def draw_offsets(key, part):
    key = jax.random.fold_in(key, 11)
    jitter = jax.random.randint(key, (WIN, SEG), 0, HOP + 1, dtype=jnp.int32)
    jitter = jitter.at[0, 0].set(0).at[0, SEG - 1].set(HOP)
    return (jnp.arange(SEG, dtype=jnp.int32)[None, :] * HOP + jitter).astype(jnp.int32)


def plant(result, key, least, largest):
    shape = result.shape
    place = [jax.random.randint(jax.random.fold_in(key, axis), (), 0, shape[axis]) for axis in range(len(shape))]
    result = result.at[tuple(place)].set(least)
    longest = shape.index(max(shape))
    place[longest] = (place[longest] + 1) % shape[longest]
    return result.at[tuple(place)].set(largest)


def shard_levels(rng, shape, split, low, top_value):
    factor_of, own = 1.0, jax.random.fold_in(rng, 6)
    for axis_at, shards_of in split:
        steps = jnp.exp(jax.random.uniform(jax.random.fold_in(own, axis_at), (shards_of,), jnp.float32, low / len(split), top_value / len(split)))
        factor_of = factor_of * jnp.repeat(steps, shape[axis_at] // shards_of).reshape([-1 if axis == axis_at else 1 for axis in range(len(shape))])
    return factor_of


def gaussian(own_key, shape, scale, limit, split=(), held_as=jnp.bfloat16):
    entries = scale * jax.random.normal(own_key, shape, jnp.float32)
    if split:
        entries = entries * shard_levels(own_key, shape, split, -0.22, 0.18)
    return jnp.clip(entries, -limit, limit).astype(held_as)


def setup_inputs(seed: int = 0) -> dict:
    seeds = jax.random.split(jax.random.key(seed), 4)
    records = gaussian(seeds[0], (WIN, C, REC), 1.0, 6.0, ((0, 4), (1, 64)))
    valid = plant((jax.random.randint(seeds[1], (WIN, C), 0, 4) < 3).astype(jnp.int32), jax.random.fold_in(seeds[1], 1), 0, 1)
    offsets = draw_offsets(jax.random.fold_in(seeds[3], 71), 0)
    return {"records": records, "valid": valid, "offsets": offsets}


def weight_values(pos, freq, part, seglen):
    posf = pos.astype(jnp.float32)
    hann = 0.5 - 0.5 * jnp.cos(2.0 * jnp.pi * posf / seglen)
    taper = hann / jnp.sqrt(jnp.float32(0.375 * seglen))
    phase = (freq * pos % seglen).astype(jnp.float32) * (2.0 * jnp.pi / seglen)
    trig = jnp.where(part == 0, jnp.cos(phase), -jnp.sin(phase))
    return taper * trig

def make_weight(first_bin, nbins, seglen):
    rows = jnp.arange(2 * nbins, dtype=jnp.int32)
    part = (rows // nbins)[:, None]
    freq = (first_bin + rows % nbins)[:, None]
    pos = jnp.arange(seglen, dtype=jnp.int32)[None, :]
    return weight_values(pos, freq, part, seglen).astype(jnp.bfloat16)

def reference(records, valid, offsets):
    weight = make_weight(BAND0, F, SEGLEN).astype(jnp.float32)

    def one_window(index):
        series = records[index]
        starts = offsets[index]
        cuts = jax.vmap(lambda start: lax.dynamic_slice_in_dim(series, start.astype(jnp.int32), SEGLEN, 1))(starts)
        spec = jnp.einsum('scn,qn->sqc', cuts.astype(jnp.float32), weight)
        spec = spec * valid[index].astype(jnp.float32)[None, None, :]
        return spec.astype(jnp.bfloat16)
    spectra = lax.map(one_window, jnp.arange(WIN, dtype=jnp.int32))
    spectra = spectra.reshape(WIN, SEG, 2, F, C).transpose(3, 0, 1, 2, 4).reshape(F, WIN * SEG, 2, C)
    scale = 1.0 / (WIN * SEG)

    def one_bin(block):
        real_part = block[:, 0].astype(jnp.float32)
        imag_part = block[:, 1].astype(jnp.float32)
        left = jnp.stack([real_part + imag_part, imag_part - real_part], axis=1).astype(jnp.bfloat16)
        product = jnp.einsum('kpr,kpc->rc', left.astype(jnp.float32), block.astype(jnp.float32))
        return (product * scale).astype(jnp.bfloat16)
    return lax.map(one_bin, spectra)
```

```python
import functools

import jax
import jax.numpy as jnp
import numpy as np
from jax import lax
from jax.experimental import pallas as pl
from jax.experimental.pallas import tpu as pltpu
from jax.sharding import PartitionSpec as P

SEGLEN = 1024
SEG = 16
BAND0 = 64
MIB = 2**20


def weight_table(nbins):
    f32 = np.float32
    rows = np.arange(2 * nbins)
    freq = (BAND0 + rows % nbins)[:, None]
    pos = np.arange(SEGLEN)[None, :]
    hann = f32(0.5) - f32(0.5) * np.cos(f32(2.0 * np.pi) * pos.astype(f32) / f32(SEGLEN))
    taper = hann / np.sqrt(f32(0.375 * SEGLEN))
    phase = (freq * pos % SEGLEN).astype(f32) * f32(2.0 * np.pi / SEGLEN)
    trig = np.where((rows < nbins)[:, None], np.cos(phase), -np.sin(phase))
    return jnp.asarray((taper * trig).astype(jnp.bfloat16))


def cut(series, start):
    tile = jnp.minimum(start // 128, 63)
    inside = start - tile * 128
    base = pl.multiple_of(tile * 128, 128)
    keep = lax.broadcasted_iota(jnp.int32, (64, 128), 1) < 128 - inside
    shift = lax.rem(128 - inside, 128)
    turned = [pltpu.roll(series[:, pl.ds(base + 128 * t, 128)], shift, 1) for t in range(9)]
    return [jnp.where(keep, turned[t], turned[t + 1]) for t in range(8)]


def spectra_kernel(offsets, records, valid, weight, out, total):
    first = lax.axis_index("panel") * 4
    for low in range(2):
        high = low + 2
        mask = jnp.concatenate(
            [valid[pl.ds(low, 1), :].astype(jnp.float32), valid[pl.ds(high, 1), :].astype(jnp.float32)], axis=1
        )

        @pl.loop(0, SEG, unroll=4)
        def _(seg):
            cuts = jnp.concatenate(
                [
                    jnp.concatenate(cut(records.at[window], offsets[first + window, seg]), axis=1)
                    for window in (low, high)
                ],
                axis=0,
            )
            spec = lax.dot_general(weight[...], cuts, (((1,), (1,)), ((), ())), preferred_element_type=jnp.float32)
            spec = spec * mask
            for part in range(2):
                row = part * 32 + seg * 2 + low
                total[pl.ds(row, 64, stride=64), :] = spec[part * 64 : (part + 1) * 64]

    @pl.loop(0, 64, unroll=8)
    def _(k):
        out[k] = total[pl.ds(pl.multiple_of(k * 64, 64), 64), :].astype(jnp.bfloat16)


def spectra(records, valid, offsets):
    return pl.pallas_call(
        spectra_kernel,
        out_shape=jax.ShapeDtypeStruct((64, 64, 128), jnp.bfloat16),
        in_specs=[pl.BlockSpec(memory_space=pltpu.SMEM)] + [pl.BlockSpec(memory_space=pltpu.VMEM)] * 3,
        out_specs=pl.BlockSpec(memory_space=pltpu.VMEM),
        scratch_shapes=[pltpu.VMEM((4096, 128), jnp.float32)],
        compiler_params=pltpu.CompilerParams(vmem_limit_bytes=48 * MIB),
    )(offsets, records, valid, weight_table(64))


def pair_rows(even, odd):
    return jnp.concatenate(
        [
            jnp.concatenate([even[:, :64], odd[:, :64]], axis=1),
            jnp.concatenate([even[:, 64:], odd[:, 64:]], axis=1),
        ],
        axis=0,
    )


def left_rows(block):
    wide = block.astype(jnp.float32)
    rows = []
    for half in range(2):
        real_part = wide[half * 64 : half * 64 + 32]
        imag_part = wide[half * 64 + 32 : half * 64 + 64]
        rows += [real_part + imag_part, imag_part - real_part]
    return jnp.concatenate(rows, axis=0).T.astype(jnp.bfloat16)


def pack_kernel(whole, right, left):
    me = lax.axis_index("panel")

    @pl.loop(0, 32)
    def _(chip):
        column = pl.multiple_of(chip * 128, 128)
        for group in range(4):
            block = pair_rows(whole[group, 2 * chip], whole[group, 2 * chip + 1])
            right[group * 128 : (group + 1) * 128, pl.ds(column, 128)] = block

            @pl.when(chip // 8 == me)
            def _():
                row = pl.multiple_of(lax.rem(chip, 8) * 128, 128)
                left[pl.ds(row, 128), group * 128 : (group + 1) * 128] = left_rows(block)


def pack(whole):
    return pl.pallas_call(
        pack_kernel,
        out_shape=(
            jax.ShapeDtypeStruct((512, 4096), jnp.bfloat16),
            jax.ShapeDtypeStruct((1024, 512), jnp.bfloat16),
        ),
        in_specs=[pl.BlockSpec(memory_space=pltpu.VMEM)],
        out_specs=(pl.BlockSpec(memory_space=pltpu.VMEM),) * 2,
        compiler_params=pltpu.CompilerParams(vmem_limit_bytes=48 * MIB),
    )(whole)


def product_kernel(left, right, out):
    total = jnp.dot(left[...], right[...], preferred_element_type=jnp.float32)
    out[...] = (total * (1.0 / 256.0)).astype(jnp.bfloat16)


def product(left, right):
    width = 256
    return pl.pallas_call(
        product_kernel,
        grid=(4096 // width,),
        out_shape=jax.ShapeDtypeStruct((1024, 4096), jnp.bfloat16),
        in_specs=[
            pl.BlockSpec((1024, 512), lambda i: (0, 0)),
            pl.BlockSpec((512, width), lambda i: (0, i)),
        ],
        out_specs=pl.BlockSpec((1024, width), lambda i: (0, i)),
        compiler_params=pltpu.CompilerParams(vmem_limit_bytes=48 * MIB),
    )(left, right)


def body(records, valid, offsets):
    blocks = spectra(records, valid, offsets)
    per_bin = lax.all_to_all(blocks, "bins", split_axis=0, concat_axis=0, tiled=True)
    whole = lax.all_gather(per_bin, "panel", axis=0)
    right, left = pack(whole)
    return product(left, right)[None]


def solution(mesh):
    placed = (P("panel", "bins", None), P("panel", "bins"), P())
    return jax.shard_map(
        body, mesh=mesh, in_specs=placed, out_specs=P("bins", "panel", None), check_vma=False
    )
```

```python
import functools

import jax
import jax.numpy as jnp
import numpy as np
from jax import lax
from jax.experimental import pallas as pl
from jax.experimental.pallas import tpu as pltpu
from jax.sharding import PartitionSpec as P

SEGLEN = 1024
SEG = 16
BAND0 = 64
MIB = 2**20
SCALE = 1.0 / 256.0
MESH = pl.DeviceIdType.MESH


def weight_table(nbins):
    f32 = np.float32
    rows = np.arange(2 * nbins)
    freq = (BAND0 + rows % nbins)[:, None]
    pos = np.arange(SEGLEN)[None, :]
    hann = f32(0.5) - f32(0.5) * np.cos(f32(2.0 * np.pi) * pos.astype(f32) / f32(SEGLEN))
    taper = hann / np.sqrt(f32(0.375 * SEGLEN))
    phase = (freq * pos % SEGLEN).astype(f32) * f32(2.0 * np.pi / SEGLEN)
    trig = np.where((rows < nbins)[:, None], np.cos(phase), -np.sin(phase))
    return jnp.asarray((taper * trig).astype(jnp.bfloat16))


def cut(series, start):
    tile = jnp.minimum(start // 128, 63)
    inside = start - tile * 128
    base = pl.multiple_of(tile * 128, 128)
    keep = lax.broadcasted_iota(jnp.int32, (64, 128), 1) < 128 - inside
    shift = lax.rem(128 - inside, 128)
    turned = [pltpu.roll(series[:, pl.ds(base + 128 * t, 128)], shift, 1) for t in range(9)]
    return [jnp.where(keep, turned[t], turned[t + 1]) for t in range(8)]


XSTEP = (0, 1, 3, 2)
ZSTEP = (0, 4, 1, 7, 3, 5, 2, 6)
STEPS = [(dx, dz) for dx in XSTEP for dz in ZSTEP]
RELAY_LAG = 6
PRODUCT_LAG = 10


def pair_rows(even, odd):
    return jnp.concatenate(
        [
            jnp.concatenate([even[:, :64], odd[:, :64]], axis=1),
            jnp.concatenate([even[:, 64:], odd[:, 64:]], axis=1),
        ],
        axis=0,
    )


def left_rows(block):
    wide = block.astype(jnp.float32)
    rows = []
    for at in range(0, 128, 32):
        real_part = wide[at : at + 16]
        imag_part = wide[at + 16 : at + 32]
        rows += [real_part + imag_part, imag_part - real_part]
    return jnp.concatenate(rows, axis=0).T.astype(jnp.bfloat16)


def spectra_kernel(offsets_in, records, valid, weight, blocks, offsets, series, mask_in, table, total, in_sems):
    me = lax.axis_index("panel")
    loads = [
        pltpu.make_async_copy(offsets_in, offsets, in_sems.at[6]),
        pltpu.make_async_copy(valid, mask_in, in_sems.at[4]),
        pltpu.make_async_copy(weight, table, in_sems.at[5]),
    ]
    reads = [pltpu.make_async_copy(records.at[w], series[w], in_sems.at[w]) for w in range(4)]
    for copy in (*loads, reads[0], reads[2], reads[1], reads[3]):
        copy.start()
    for copy in loads:
        copy.wait()

    for low in range(2):
        reads[low].wait()
        reads[low + 2].wait()
        mask = jnp.concatenate(
            [mask_in[w : w + 1, :].astype(jnp.float32) for w in (low, low + 2)], axis=1
        )

        @pl.loop(0, SEG, unroll=4)
        def _(seg):
            cuts = jnp.concatenate(
                [
                    jnp.concatenate(cut(series[w], offsets[me * 4 + w, seg]), axis=1)
                    for w in (low, low + 2)
                ],
                axis=0,
            )
            spec = lax.dot_general(table[...], cuts, (((1,), (1,)), ((), ())), preferred_element_type=jnp.float32)
            spec = spec * mask
            for part in range(2):
                row = low * 32 + part * 16 + seg
                total[pl.ds(row, 64, stride=64), :] = spec[part * 64 : (part + 1) * 64]

    @pl.loop(0, 64, unroll=8)
    def _(k):
        blocks[k] = total[pl.ds(pl.multiple_of(k * 64, 64), 64), :].astype(jnp.bfloat16)


def spectra(records, valid, offsets):
    bf16 = jnp.bfloat16
    return pl.pallas_call(
        spectra_kernel,
        out_shape=pltpu.VMEM((64, 64, 128), bf16),
        in_specs=[pl.BlockSpec(memory_space=pltpu.HBM)] * 4,
        out_specs=pl.BlockSpec(memory_space=pltpu.VMEM),
        scratch_shapes=[
            pltpu.SMEM((16, 16), jnp.int32),
            [pltpu.VMEM((64, 9216), bf16) for _ in range(4)],
            pltpu.VMEM((4, 64), jnp.int32),
            pltpu.VMEM((128, SEGLEN), bf16),
            pltpu.VMEM((4096, 128), jnp.float32),
            pltpu.SemaphoreType.DMA((7,)),
        ],
        compiler_params=pltpu.CompilerParams(vmem_limit_bytes=36 * MIB),
    )(*(pltpu.with_memory_space_constraint(a, pltpu.HBM) for a in (offsets, records, valid, weight_table(64))))


def main_kernel(
    blocks, right, left, whole,
    own_sem, plane_send, plane_recv, ring_send, ring_recv, relay_send, relay_recv,
):
    b = lax.axis_index("bins")
    me = lax.axis_index("panel")
    x, z, core = b // 16, lax.rem(b // 2, 8), lax.rem(b, 2)
    chip = b // 2
    up, down, across = lax.rem(me + 1, 4), lax.rem(me + 3, 4), lax.rem(me + 2, 4)

    barrier = pltpu.get_barrier_semaphore()

    @pl.loop(1, 64)
    def _(i):
        pl.semaphore_signal(barrier, inc=1, device_id={"bins": lax.rem(b + i, 64)}, device_id_type=MESH)

    for there in (up, down):
        pl.semaphore_signal(barrier, inc=1, device_id={"panel": there}, device_id_type=MESH)

    pl.semaphore_wait(barrier, 65)

    own = pltpu.make_async_copy(blocks.at[b], whole.at[me, b], own_sem)
    own.start()

    def send(dx, dz, there_core):
        there = (lax.rem(x + dx, 4) * 8 + lax.rem(z + dz, 8)) * 2 + there_core
        pltpu.make_async_remote_copy(
            blocks.at[there], whole.at[me, b], plane_send, plane_recv.at[chip],
            device_id={"bins": there}, device_id_type=MESH,
        ).start()

    for dx, dz in STEPS:
        if (dx, dz) != (0, 0):
            send(dx, dz, core)
        send(dx, dz, 1 - core)
    own.wait()

    def source(step):
        dx, dz = STEPS[step]
        return lax.rem(x + 4 - dx, 4) * 8 + lax.rem(z + 8 - dz, 8)

    def chunk(group, k, there, send_sem, recv_sem):
        part = whole.at[group, pl.ds(2 * k, 2)]
        return pltpu.make_async_remote_copy(
            part, part, send_sem, recv_sem, device_id={"panel": there}, device_id_type=MESH
        )

    def plane_arrival(step):
        n = 2 if step else 1
        part = blocks.at[pl.ds(0, n)]
        pltpu.make_async_remote_copy(
            part, part, plane_send, plane_recv.at[source(step)], device_id={"bins": b}, device_id_type=MESH
        ).wait_recv()

    def forward(step):
        k = source(step)
        chunk(me, k, up, ring_send, ring_recv.at[0, k]).start()
        chunk(me, k, down, ring_send, ring_recv.at[1, k]).start()

    def relay(step):
        k = source(step)
        chunk(down, k, up, ring_send, ring_recv.at[0, k]).wait_recv()
        chunk(up, k, down, ring_send, ring_recv.at[1, k]).wait_recv()
        if step % 2 == 0:
            chunk(down, k, up, relay_send, relay_recv.at[k]).start()
        else:
            chunk(up, k, down, relay_send, relay_recv.at[k]).start()

    def use(step):
        k = source(step)
        chunk(across, k, up, relay_send, relay_recv.at[k]).wait_recv()
        column = pl.ds(pl.multiple_of(k * 128, 128), 128)
        for group in range(4):
            rows = slice(group * 128, (group + 1) * 128)
            block = pair_rows(whole[group, 2 * k], whole[group, 2 * k + 1])
            right[rows, column] = block

        @pl.when(k // 8 == me)
        def _():
            place = pl.ds(pl.multiple_of(lax.rem(k, 8) * 128, 128), 128)
            for group in range(4):
                rows = slice(group * 128, (group + 1) * 128)
                left[place, rows] = left_rows(right[rows, column])

    last = len(STEPS)
    for step in range(last + PRODUCT_LAG):
        if step < last:
            plane_arrival(step)
            forward(step)
        if 0 <= step - RELAY_LAG < last:
            relay(step - RELAY_LAG)
        if step >= PRODUCT_LAG:
            use(step - PRODUCT_LAG)

    def sent(part, sem):
        pltpu.make_async_remote_copy(
            part, part, sem, relay_recv.at[0], device_id={"panel": up}, device_id_type=MESH
        ).wait_send()

    sent(blocks.at[pl.ds(0, 63)], plane_send)
    sent(whole.at[pl.ds(0, 2)], ring_send)
    sent(whole.at[0], relay_send)


def main(blocks):
    dma = pltpu.SemaphoreType.DMA
    bf16 = jnp.bfloat16
    return pl.pallas_call(
        main_kernel,
        out_shape=(pltpu.VMEM((512, 4096), bf16), pltpu.VMEM((1024, 512), bf16)),
        in_specs=[pl.BlockSpec(memory_space=pltpu.VMEM)],
        out_specs=(pl.BlockSpec(memory_space=pltpu.VMEM),) * 2,
        scratch_shapes=[
            pltpu.VMEM((4, 64, 64, 128), bf16),
            dma(()), dma(()), dma((32,)), dma(()), dma((2, 32)), dma(()), dma((32,)),
        ],
        compiler_params=pltpu.CompilerParams(
            collective_id=0, has_side_effects=True, vmem_limit_bytes=36 * MIB
        ),
        cost_estimate=pl.CostEstimate(flops=10**10, bytes_accessed=2 * 10**7, transcendentals=0),
    )(pltpu.with_memory_space_constraint(blocks, pltpu.VMEM))


def product_kernel(right, left, out, result, sems):
    copies = []
    for at in range(8):
        wide = pl.ds(at * 512, 512)
        part = jnp.dot(left[...], right[:, wide], preferred_element_type=jnp.float32)
        result[:, wide] = (part * SCALE).astype(jnp.bfloat16)
        copies.append(pltpu.make_async_copy(result.at[:, wide], out.at[:, wide], sems.at[at]))
        copies[-1].start()
    for copy in copies:
        copy.wait()


def product(right, left):
    return pl.pallas_call(
        product_kernel,
        out_shape=jax.ShapeDtypeStruct((1024, 4096), jnp.bfloat16),
        in_specs=[pl.BlockSpec(memory_space=pltpu.VMEM)] * 2,
        out_specs=pl.BlockSpec(memory_space=pl.ANY),
        scratch_shapes=[pltpu.VMEM((1024, 4096), jnp.bfloat16), pltpu.SemaphoreType.DMA((8,))],
        compiler_params=pltpu.CompilerParams(vmem_limit_bytes=36 * MIB),
    )(*(pltpu.with_memory_space_constraint(a, pltpu.VMEM) for a in (right, left)))


def body(records, valid, offsets):
    return product(*main(spectra(records, valid, offsets)))[None]


def solution(mesh):
    placed = (P("panel", "bins", None), P("panel", "bins"), P())
    return jax.shard_map(
        body, mesh=mesh, in_specs=placed, out_specs=P("bins", "panel", None), check_vma=False
    )
```

```python
import functools

import jax
import jax.numpy as jnp
import numpy as np
from jax import lax
from jax.experimental import pallas as pl
from jax.experimental.pallas import tpu as pltpu
from jax.sharding import PartitionSpec as P

SEGLEN = 1024
SEG = 16
BAND0 = 64
MIB = 2**20
SCALE = 1.0 / 256.0
MESH = pl.DeviceIdType.MESH


def weight_table(nbins):
    f32 = np.float32
    rows = np.arange(2 * nbins)
    freq = (BAND0 + rows % nbins)[:, None]
    pos = np.arange(SEGLEN)[None, :]
    hann = f32(0.5) - f32(0.5) * np.cos(f32(2.0 * np.pi) * pos.astype(f32) / f32(SEGLEN))
    taper = hann / np.sqrt(f32(0.375 * SEGLEN))
    phase = (freq * pos % SEGLEN).astype(f32) * f32(2.0 * np.pi / SEGLEN)
    trig = np.where((rows < nbins)[:, None], np.cos(phase), -np.sin(phase))
    return jnp.asarray((taper * trig).astype(jnp.bfloat16))


def cut(series, start):
    tile = jnp.minimum(start // 128, 63)
    inside = start - tile * 128
    base = pl.multiple_of(tile * 128, 128)
    keep = lax.broadcasted_iota(jnp.int32, (64, 128), 1) < 128 - inside
    shift = lax.rem(128 - inside, 128)
    turned = [pltpu.roll(series[:, pl.ds(base + 128 * t, 128)], shift, 1) for t in range(9)]
    return [jnp.where(keep, turned[t], turned[t + 1]) for t in range(8)]


XSTEP = (0, 1, 3, 2)
ZSTEP = (0, 1, 7, 2, 6, 3, 5, 4)
STEPS = [(dx, dz) for dx in XSTEP for dz in ZSTEP]
RELAY_LAG = 6
PRODUCT_LAG = 10
EARLY = 8


def pair_rows(even, odd):
    return jnp.concatenate(
        [
            jnp.concatenate([even[:, :64], odd[:, :64]], axis=1),
            jnp.concatenate([even[:, 64:], odd[:, 64:]], axis=1),
        ],
        axis=0,
    )


def left_rows(block):
    wide = block.astype(jnp.float32)
    rows = []
    for at in range(0, 128, 32):
        real_part = wide[at : at + 16]
        imag_part = wide[at + 16 : at + 32]
        rows += [real_part + imag_part, imag_part - real_part]
    return jnp.concatenate(rows, axis=0).T.astype(jnp.bfloat16)


def cuts_kernel(offsets_in, records, valid, weight, cuts, table, mask, offsets, series, mask_in, in_sems):
    me = lax.axis_index("panel")
    load = pltpu.make_async_copy(offsets_in, offsets, in_sems.at[8])
    load.start()
    reads = []
    for part, (first, count) in enumerate(((0, 5248), (5248, 3968))):
        for low in range(2):
            for w in (low, low + 2):
                place = pl.ds(first, count)
                reads.append(
                    pltpu.make_async_copy(records.at[w, :, place], series[w].at[:, place], in_sems.at[part * 4 + w])
                )
    others = [
        pltpu.make_async_copy(valid, mask_in, in_sems.at[9]),
        pltpu.make_async_copy(weight, table, in_sems.at[10]),
    ]
    for copy in (*reads, *others):
        copy.start()
    load.wait()
    for part in range(2):
        for low in range(2):
            for copy in reads[part * 4 + low * 2 : part * 4 + low * 2 + 2]:
                copy.wait()

            @pl.loop(part * 8, part * 8 + 8, unroll=4)
            def _(seg):
                for half in range(2):
                    w = low + 2 * half
                    tiles = cut(series[w], offsets[me * 4 + w, seg])
                    for t in range(8):
                        cuts[low * SEG + seg, half * 64 : half * 64 + 64, t * 128 : t * 128 + 128] = tiles[t]

    for copy in others:
        copy.wait()
    for low in range(2):
        mask[low : low + 1, :] = jnp.concatenate(
            [mask_in[w : w + 1, :].astype(jnp.float32) for w in (low, low + 2)], axis=1
        )


def segments(records, valid, offsets):
    bf16 = jnp.bfloat16
    return pl.pallas_call(
        cuts_kernel,
        out_shape=(
            pltpu.VMEM((2 * SEG, 128, SEGLEN), bf16),
            pltpu.VMEM((128, SEGLEN), bf16),
            pltpu.VMEM((2, 128), jnp.float32),
        ),
        in_specs=[pl.BlockSpec(memory_space=pltpu.HBM)] * 4,
        out_specs=(pl.BlockSpec(memory_space=pltpu.VMEM),) * 3,
        scratch_shapes=[
            pltpu.SMEM((16, 16), jnp.int32),
            [pltpu.VMEM((64, 9216), bf16) for _ in range(4)],
            pltpu.VMEM((4, 64), jnp.int32),
            pltpu.SemaphoreType.DMA((11,)),
        ],
        compiler_params=pltpu.CompilerParams(vmem_limit_bytes=32 * MIB),
    )(*(pltpu.with_memory_space_constraint(a, pltpu.HBM) for a in (offsets, records, valid, weight_table(64))))


def main_kernel(
    cuts, table, mask, right, left, total, blocks, whole,
    own_sem, plane_send, plane_recv, ring_send, ring_recv, relay_send, relay_recv,
):
    b = lax.axis_index("bins")
    me = lax.axis_index("panel")
    x, z, core = b // 16, lax.rem(b // 2, 8), lax.rem(b, 2)
    chip = b // 2
    up, down, across = lax.rem(me + 1, 4), lax.rem(me + 3, 4), lax.rem(me + 2, 4)

    barrier = pltpu.get_barrier_semaphore()

    @pl.loop(1, 64)
    def _(i):
        pl.semaphore_signal(barrier, inc=1, device_id={"bins": lax.rem(b + i, 64)}, device_id_type=MESH)

    for there in (up, down):
        pl.semaphore_signal(barrier, inc=1, device_id={"panel": there}, device_id_type=MESH)

    def spectra(low):
        keep = mask[low : low + 1, :]

        @pl.loop(0, SEG, unroll=4)
        def _(seg):
            spec = lax.dot_general(
                table[...], cuts[low * SEG + seg], (((1,), (1,)), ((), ())), preferred_element_type=jnp.float32
            )
            spec = spec * keep
            for part in range(2):
                total[pl.ds(part * 16 + seg, 64, stride=32), :] = spec[part * 64 : (part + 1) * 64]

        @pl.loop(0, 64, unroll=8)
        def _(k):
            blocks[k, low * 32 : low * 32 + 32] = total[pl.ds(pl.multiple_of(k * 32, 32), 32), :].astype(jnp.bfloat16)

    def send(step, first, count):
        dx, dz = STEPS[step]
        rows = pl.ds(first, count)
        for there_core in (core, 1 - core) if step else (1 - core,):
            there = (lax.rem(x + dx, 4) * 8 + lax.rem(z + dz, 8)) * 2 + there_core
            pltpu.make_async_remote_copy(
                blocks.at[there, rows], whole.at[me, b, rows], plane_send, plane_recv.at[chip],
                device_id={"bins": there}, device_id_type=MESH,
            ).start()

    spectra(0)
    pl.semaphore_wait(barrier, 65)
    for step in range(EARLY):
        send(step, 0, 32)
    spectra(1)
    own = pltpu.make_async_copy(blocks.at[b], whole.at[me, b], own_sem)
    own.start()
    for step in range(EARLY):
        send(step, 32, 32)
    for step in range(EARLY, len(STEPS)):
        send(step, 0, 64)
    own.wait()

    def source(step):
        dx, dz = STEPS[step]
        return lax.rem(x + 4 - dx, 4) * 8 + lax.rem(z + 8 - dz, 8)

    def chunk(group, k, there, send_sem, recv_sem):
        part = whole.at[group, pl.ds(2 * k, 2)]
        return pltpu.make_async_remote_copy(
            part, part, send_sem, recv_sem, device_id={"panel": there}, device_id_type=MESH
        )

    def plane_arrival(step):
        n = 2 if step else 1
        part = blocks.at[pl.ds(0, n)]
        pltpu.make_async_remote_copy(
            part, part, plane_send, plane_recv.at[source(step)], device_id={"bins": b}, device_id_type=MESH
        ).wait_recv()

    def forward(step):
        k = source(step)
        chunk(me, k, up, ring_send, ring_recv.at[0, k]).start()
        chunk(me, k, down, ring_send, ring_recv.at[1, k]).start()

    def relay(step):
        k = source(step)
        chunk(down, k, up, ring_send, ring_recv.at[0, k]).wait_recv()
        chunk(up, k, down, ring_send, ring_recv.at[1, k]).wait_recv()
        if step % 2 == 0:
            chunk(down, k, up, relay_send, relay_recv.at[k]).start()
        else:
            chunk(up, k, down, relay_send, relay_recv.at[k]).start()

    def use(step):
        k = source(step)
        chunk(across, k, up, relay_send, relay_recv.at[k]).wait_recv()
        column = pl.ds(pl.multiple_of(k * 128, 128), 128)
        for group in range(4):
            rows = slice(group * 128, (group + 1) * 128)
            block = pair_rows(whole[group, 2 * k], whole[group, 2 * k + 1])
            right[rows, column] = block

        @pl.when(k // 8 == me)
        def _():
            place = pl.ds(pl.multiple_of(lax.rem(k, 8) * 128, 128), 128)
            for group in range(4):
                rows = slice(group * 128, (group + 1) * 128)
                left[place, rows] = left_rows(right[rows, column])

    last = len(STEPS)
    for step in range(last + PRODUCT_LAG):
        if step < last:
            plane_arrival(step)
            forward(step)
        if 0 <= step - RELAY_LAG < last:
            relay(step - RELAY_LAG)
        if step >= PRODUCT_LAG:
            use(step - PRODUCT_LAG)

    def sent(part, sem):
        pltpu.make_async_remote_copy(
            part, part, sem, relay_recv.at[0], device_id={"panel": up}, device_id_type=MESH
        ).wait_send()

    sent(blocks.at[pl.ds(0, 63)], plane_send)
    sent(whole.at[pl.ds(0, 2)], ring_send)
    sent(whole.at[0], relay_send)


def main(cuts, table, mask):
    dma = pltpu.SemaphoreType.DMA
    bf16 = jnp.bfloat16
    return pl.pallas_call(
        main_kernel,
        out_shape=(pltpu.VMEM((512, 4096), bf16), pltpu.VMEM((1024, 512), bf16)),
        in_specs=[pl.BlockSpec(memory_space=pltpu.VMEM)] * 3,
        out_specs=(pl.BlockSpec(memory_space=pltpu.VMEM),) * 2,
        scratch_shapes=[
            pltpu.VMEM((64 * 32, 128), jnp.float32),
            pltpu.VMEM((64, 64, 128), bf16),
            pltpu.VMEM((4, 64, 64, 128), bf16),
            dma(()), dma(()), dma((32,)), dma(()), dma((2, 32)), dma(()), dma((32,)),
        ],
        compiler_params=pltpu.CompilerParams(
            collective_id=0, has_side_effects=True, vmem_limit_bytes=32 * MIB
        ),
        cost_estimate=pl.CostEstimate(flops=10**10, bytes_accessed=2 * 10**7, transcendentals=0),
    )(*(pltpu.with_memory_space_constraint(a, pltpu.VMEM) for a in (cuts, table, mask)))


def product_kernel(right, left, out, result, sems):
    copies = []
    for at in range(8):
        wide = pl.ds(at * 512, 512)
        part = jnp.dot(left[...], right[:, wide], preferred_element_type=jnp.float32)
        result[:, wide] = (part * SCALE).astype(jnp.bfloat16)
        copies.append(pltpu.make_async_copy(result.at[:, wide], out.at[:, wide], sems.at[at]))
        copies[-1].start()
    for copy in copies:
        copy.wait()


def product(right, left):
    return pl.pallas_call(
        product_kernel,
        out_shape=jax.ShapeDtypeStruct((1024, 4096), jnp.bfloat16),
        in_specs=[pl.BlockSpec(memory_space=pltpu.VMEM)] * 2,
        out_specs=pl.BlockSpec(memory_space=pl.ANY),
        scratch_shapes=[pltpu.VMEM((1024, 4096), jnp.bfloat16), pltpu.SemaphoreType.DMA((8,))],
        compiler_params=pltpu.CompilerParams(vmem_limit_bytes=32 * MIB),
    )(*(pltpu.with_memory_space_constraint(a, pltpu.VMEM) for a in (right, left)))


def body(records, valid, offsets):
    return product(*main(*segments(records, valid, offsets)))[None]


def solution(mesh):
    placed = (P("panel", "bins", None), P("panel", "bins"), P())
    return jax.shard_map(
        body, mesh=mesh, in_specs=placed, out_specs=P("bins", "panel", None), check_vma=False
    )
```

```python
import functools

import jax
import jax.numpy as jnp
import numpy as np
from jax import lax
from jax.experimental import pallas as pl
from jax.experimental.pallas import tpu as pltpu
from jax.sharding import PartitionSpec as P

SEGLEN = 1024
SEG = 16
BAND0 = 64
MIB = 2**20
SCALE = 1.0 / 256.0
MESH = pl.DeviceIdType.MESH


def weight_table(nbins):
    f32 = np.float32
    rows = np.arange(2 * nbins)
    freq = (BAND0 + rows % nbins)[:, None]
    pos = np.arange(SEGLEN)[None, :]
    hann = f32(0.5) - f32(0.5) * np.cos(f32(2.0 * np.pi) * pos.astype(f32) / f32(SEGLEN))
    taper = hann / np.sqrt(f32(0.375 * SEGLEN))
    phase = (freq * pos % SEGLEN).astype(f32) * f32(2.0 * np.pi / SEGLEN)
    trig = np.where((rows < nbins)[:, None], np.cos(phase), -np.sin(phase))
    return jnp.asarray((taper * trig).astype(jnp.bfloat16))


def cut(series, start):
    tile = jnp.minimum(start // 128, 63)
    inside = start - tile * 128
    base = pl.multiple_of(tile * 128, 128)
    keep = lax.broadcasted_iota(jnp.int32, (64, 128), 1) < 128 - inside
    shift = lax.rem(128 - inside, 128)
    turned = [pltpu.roll(series[:, pl.ds(base + 128 * t, 128)], shift, 1) for t in range(9)]
    return [jnp.where(keep, turned[t], turned[t + 1]) for t in range(8)]


XSTEP = (0, 1, 3, 2)
ZSTEP = (0, 1, 7, 2, 6, 3, 5, 4)
STEPS = [(dx, dz) for dx in XSTEP for dz in ZSTEP]
RELAY_LAG = 6
PRODUCT_LAG = 10
EARLY = 8


def pair_rows(even, odd):
    return jnp.concatenate(
        [
            jnp.concatenate([even[:, :64], odd[:, :64]], axis=1),
            jnp.concatenate([even[:, 64:], odd[:, 64:]], axis=1),
        ],
        axis=0,
    )


def left_rows(block):
    wide = block.astype(jnp.float32)
    rows = []
    for at in range(0, 128, 32):
        real_part = wide[at : at + 16]
        imag_part = wide[at + 16 : at + 32]
        rows += [real_part + imag_part, imag_part - real_part]
    return jnp.concatenate(rows, axis=0).T.astype(jnp.bfloat16)


def cuts_kernel(offsets_in, records, valid, weight, cuts, table, mask, offsets, series, mask_in, in_sems):
    me = lax.axis_index("panel")
    load = pltpu.make_async_copy(offsets_in, offsets, in_sems.at[8])
    load.start()
    reads = []
    for part, (first, count) in enumerate(((0, 5248), (5248, 3968))):
        for low in range(2):
            for w in (low, low + 2):
                place = pl.ds(first, count)
                reads.append(
                    pltpu.make_async_copy(records.at[w, :, place], series[w].at[:, place], in_sems.at[part * 4 + w])
                )
    others = [
        pltpu.make_async_copy(valid, mask_in, in_sems.at[9]),
        pltpu.make_async_copy(weight, table, in_sems.at[10]),
    ]
    for copy in (*reads, *others):
        copy.start()
    load.wait()
    for part in range(2):
        for low in range(2):
            for copy in reads[part * 4 + low * 2 : part * 4 + low * 2 + 2]:
                copy.wait()

            @pl.loop(part * 8, part * 8 + 8, unroll=4)
            def _(seg):
                for half in range(2):
                    w = low + 2 * half
                    tiles = cut(series[w], offsets[me * 4 + w, seg])
                    for t in range(8):
                        cuts[low * SEG + seg, half * 64 : half * 64 + 64, t * 128 : t * 128 + 128] = tiles[t]

    for copy in others:
        copy.wait()
    for low in range(2):
        mask[low : low + 1, :] = jnp.concatenate(
            [mask_in[w : w + 1, :].astype(jnp.float32) for w in (low, low + 2)], axis=1
        )


def segments(records, valid, offsets):
    bf16 = jnp.bfloat16
    return pl.pallas_call(
        cuts_kernel,
        out_shape=(
            pltpu.VMEM((2 * SEG, 128, SEGLEN), bf16),
            pltpu.VMEM((128, SEGLEN), bf16),
            pltpu.VMEM((2, 128), jnp.float32),
        ),
        in_specs=[pl.BlockSpec(memory_space=pltpu.HBM)] * 4,
        out_specs=(pl.BlockSpec(memory_space=pltpu.VMEM),) * 3,
        scratch_shapes=[
            pltpu.SMEM((16, 16), jnp.int32),
            [pltpu.VMEM((64, 9216), bf16) for _ in range(4)],
            pltpu.VMEM((4, 64), jnp.int32),
            pltpu.SemaphoreType.DMA((11,)),
        ],
        compiler_params=pltpu.CompilerParams(vmem_limit_bytes=32 * MIB),
    )(*(pltpu.with_memory_space_constraint(a, pltpu.HBM) for a in (offsets, records, valid, weight_table(64))))


def main_kernel(
    cuts, table, mask, right, left, early, total, blocks, whole,
    own_sem, plane_send, plane_recv, ring_send, ring_recv, relay_send, relay_recv,
):
    b = lax.axis_index("bins")
    me = lax.axis_index("panel")
    x, z, core = b // 16, lax.rem(b // 2, 8), lax.rem(b, 2)
    chip = b // 2
    up, down, across = lax.rem(me + 1, 4), lax.rem(me + 3, 4), lax.rem(me + 2, 4)

    barrier = pltpu.get_barrier_semaphore()

    @pl.loop(1, 64)
    def _(i):
        pl.semaphore_signal(barrier, inc=1, device_id={"bins": lax.rem(b + i, 64)}, device_id_type=MESH)

    for there in (up, down):
        pl.semaphore_signal(barrier, inc=1, device_id={"panel": there}, device_id_type=MESH)

    def spectra(low):
        keep = mask[low : low + 1, :]

        @pl.loop(0, SEG, unroll=4)
        def _(seg):
            spec = lax.dot_general(
                table[...], cuts[low * SEG + seg], (((1,), (1,)), ((), ())), preferred_element_type=jnp.float32
            )
            spec = spec * keep
            for part in range(2):
                total[pl.ds(part * 16 + seg, 64, stride=32), :] = spec[part * 64 : (part + 1) * 64]

        @pl.loop(0, 64, unroll=8)
        def _(k):
            blocks[k, low * 32 : low * 32 + 32] = total[pl.ds(pl.multiple_of(k * 32, 32), 32), :].astype(jnp.bfloat16)

    def send(step, first, count):
        dx, dz = STEPS[step]
        rows = pl.ds(first, count)
        for there_core in (core, 1 - core) if step else (1 - core,):
            there = (lax.rem(x + dx, 4) * 8 + lax.rem(z + dz, 8)) * 2 + there_core
            pltpu.make_async_remote_copy(
                blocks.at[there, rows], whole.at[me, b, rows], plane_send, plane_recv.at[chip],
                device_id={"bins": there}, device_id_type=MESH,
            ).start()

    spectra(0)
    pl.semaphore_wait(barrier, 65)
    for step in range(EARLY):
        send(step, 0, 32)
    spectra(1)
    own = pltpu.make_async_copy(blocks.at[b], whole.at[me, b], own_sem)
    own.start()
    for step in range(EARLY):
        send(step, 32, 32)
    for step in range(EARLY, len(STEPS)):
        send(step, 0, 64)
    own.wait()

    def source(step):
        dx, dz = STEPS[step]
        return lax.rem(x + 4 - dx, 4) * 8 + lax.rem(z + 8 - dz, 8)

    def chunk(group, k, there, send_sem, recv_sem):
        part = whole.at[group, pl.ds(2 * k, 2)]
        return pltpu.make_async_remote_copy(
            part, part, send_sem, recv_sem, device_id={"panel": there}, device_id_type=MESH
        )

    def plane_arrival(step):
        n = 2 if step else 1
        part = blocks.at[pl.ds(0, n)]
        pltpu.make_async_remote_copy(
            part, part, plane_send, plane_recv.at[source(step)], device_id={"bins": b}, device_id_type=MESH
        ).wait_recv()

    def forward(step):
        k = source(step)
        chunk(me, k, up, ring_send, ring_recv.at[0, k]).start()
        chunk(me, k, down, ring_send, ring_recv.at[1, k]).start()

    def relay(step):
        k = source(step)
        chunk(down, k, up, ring_send, ring_recv.at[0, k]).wait_recv()
        chunk(up, k, down, ring_send, ring_recv.at[1, k]).wait_recv()
        if step % 2 == 0:
            chunk(down, k, up, relay_send, relay_recv.at[k]).start()
        else:
            chunk(up, k, down, relay_send, relay_recv.at[k]).start()

    def use(step):
        k = source(step)
        chunk(across, k, up, relay_send, relay_recv.at[k]).wait_recv()
        column = pl.ds(pl.multiple_of(k * 128, 128), 128)
        for group in range(4):
            rows = slice(group * 128, (group + 1) * 128)
            block = pair_rows(whole[group, 2 * k], whole[group, 2 * k + 1])
            right[rows, column] = block

        turned = (2 - STEPS[step][1]) % 8 * 128

        @pl.when(k // 8 == me)
        def _():
            for group in range(4):
                rows = slice(group * 128, (group + 1) * 128)
                left[turned : turned + 128, rows] = left_rows(right[rows, column])

    def multiply_early(slab):
        first = lax.rem(x + 4 - XSTEP[slab], 4) * 1024
        for half in range(2):
            wide = pl.ds(pl.multiple_of(first + half * 512, 512), 512)
            part = jnp.dot(left[:512, :], right[:, wide], preferred_element_type=jnp.float32)
            place = slab * 1024 + half * 512
            early[:, place : place + 512] = (part * SCALE).astype(jnp.bfloat16)

    last = len(STEPS)
    for step in range(last + PRODUCT_LAG):
        if step < last:
            plane_arrival(step)
            forward(step)
        if 0 <= step - RELAY_LAG < last:
            relay(step - RELAY_LAG)
        if step >= PRODUCT_LAG:
            use(step - PRODUCT_LAG)
            if 0 <= step - PRODUCT_LAG - 27 < 3:
                multiply_early(step - PRODUCT_LAG - 27)

    def sent(part, sem):
        pltpu.make_async_remote_copy(
            part, part, sem, relay_recv.at[0], device_id={"panel": up}, device_id_type=MESH
        ).wait_send()

    sent(blocks.at[pl.ds(0, 63)], plane_send)
    sent(whole.at[pl.ds(0, 2)], ring_send)
    sent(whole.at[0], relay_send)


def main(cuts, table, mask):
    dma = pltpu.SemaphoreType.DMA
    bf16 = jnp.bfloat16
    return pl.pallas_call(
        main_kernel,
        out_shape=(
            pltpu.VMEM((512, 4096), bf16),
            pltpu.VMEM((1024, 512), bf16),
            pltpu.VMEM((512, 3072), bf16),
        ),
        in_specs=[pl.BlockSpec(memory_space=pltpu.VMEM)] * 3,
        out_specs=(pl.BlockSpec(memory_space=pltpu.VMEM),) * 3,
        scratch_shapes=[
            pltpu.VMEM((64 * 32, 128), jnp.float32),
            pltpu.VMEM((64, 64, 128), bf16),
            pltpu.VMEM((4, 64, 64, 128), bf16),
            dma(()), dma(()), dma((32,)), dma(()), dma((2, 32)), dma(()), dma((32,)),
        ],
        compiler_params=pltpu.CompilerParams(
            collective_id=0, has_side_effects=True, vmem_limit_bytes=32 * MIB
        ),
        cost_estimate=pl.CostEstimate(flops=10**10, bytes_accessed=2 * 10**7, transcendentals=0),
    )(*(pltpu.with_memory_space_constraint(a, pltpu.VMEM) for a in (cuts, table, mask)))


def product_kernel(right, left, early, out, result, sems):
    b = lax.axis_index("bins")
    x, z = b // 16, lax.rem(b // 2, 8)
    copies = []

    def store(held, slab, half):
        first = pl.multiple_of(lax.rem(x + 4 - XSTEP[slab], 4) * 1024, 1024)
        for at in range(half * 4, half * 4 + 4):
            row = pl.multiple_of(lax.rem(z + 6 + at, 8) * 128, 128)
            copies.append(
                pltpu.make_async_copy(
                    held.at[pl.ds(at * 128, 128), pl.ds(slab * 1024, 1024)],
                    out.at[pl.ds(row, 128), pl.ds(first, 1024)],
                    sems.at[slab, at],
                )
            )
            copies[-1].start()

    def multiply(slab, half):
        first = lax.rem(x + 4 - XSTEP[slab], 4) * 1024
        rows = pl.ds(half * 512, 512)
        for at in range(2):
            wide = pl.ds(pl.multiple_of(first + at * 512, 512), 512)
            part = jnp.dot(left[rows, :], right[:, wide], preferred_element_type=jnp.float32)
            result[rows, pl.ds(slab * 1024 + at * 512, 512)] = (part * SCALE).astype(jnp.bfloat16)
        store(result, slab, half)

    for slab in range(3):
        store(early, slab, 0)
    multiply(3, 0)
    for slab in range(4):
        multiply(slab, 1)
    for copy in copies:
        copy.wait()


def product(right, left, early):
    return pl.pallas_call(
        product_kernel,
        out_shape=jax.ShapeDtypeStruct((1024, 4096), jnp.bfloat16),
        in_specs=[pl.BlockSpec(memory_space=pltpu.VMEM)] * 3,
        out_specs=pl.BlockSpec(memory_space=pl.ANY),
        scratch_shapes=[pltpu.VMEM((1024, 4096), jnp.bfloat16), pltpu.SemaphoreType.DMA((4, 8))],
        compiler_params=pltpu.CompilerParams(vmem_limit_bytes=32 * MIB),
    )(*(pltpu.with_memory_space_constraint(a, pltpu.VMEM) for a in (right, left, early)))


def body(records, valid, offsets):
    return product(*main(*segments(records, valid, offsets)))[None]


def solution(mesh):
    placed = (P("panel", "bins", None), P("panel", "bins"), P())
    return jax.shard_map(
        body, mesh=mesh, in_specs=placed, out_specs=P("bins", "panel", None), check_vma=False
    )
```

```python
import functools

import jax
import jax.numpy as jnp
import numpy as np
from jax import lax
from jax.experimental import pallas as pl
from jax.experimental.pallas import tpu as pltpu
from jax.sharding import PartitionSpec as P

SEGLEN = 1024
SEG = 16
BAND0 = 64
MIB = 2**20
SCALE = 1.0 / 256.0
MESH = pl.DeviceIdType.MESH


def weight_table(nbins):
    f32 = np.float32
    rows = np.arange(2 * nbins)
    freq = (BAND0 + rows % nbins)[:, None]
    pos = np.arange(SEGLEN)[None, :]
    hann = f32(0.5) - f32(0.5) * np.cos(f32(2.0 * np.pi) * pos.astype(f32) / f32(SEGLEN))
    taper = hann / np.sqrt(f32(0.375 * SEGLEN))
    phase = (freq * pos % SEGLEN).astype(f32) * f32(2.0 * np.pi / SEGLEN)
    trig = np.where((rows < nbins)[:, None], np.cos(phase), -np.sin(phase))
    return jnp.asarray((taper * trig).astype(jnp.bfloat16))


def cut(series, start):
    tile = jnp.minimum(start // 128, 63)
    inside = start - tile * 128
    base = pl.multiple_of(tile * 128, 128)
    keep = lax.broadcasted_iota(jnp.int32, (64, 128), 1) < 128 - inside
    shift = lax.rem(128 - inside, 128)
    turned = [pltpu.roll(series[:, pl.ds(base + 128 * t, 128)], shift, 1) for t in range(9)]
    return [jnp.where(keep, turned[t], turned[t + 1]) for t in range(8)]


XSTEP = (0, 1, 3, 2)
ZSTEP = (0, 1, 7, 2, 6, 3, 5, 4)
STEPS = [(dx, dz) for dx in XSTEP for dz in ZSTEP]
RELAY_LAG = 6
PRODUCT_LAG = 10
EARLY = 8
DIRECT = (8, 16, 24)


def pair_rows(even, odd):
    return jnp.concatenate(
        [
            jnp.concatenate([even[:, :64], odd[:, :64]], axis=1),
            jnp.concatenate([even[:, 64:], odd[:, 64:]], axis=1),
        ],
        axis=0,
    )


def left_rows(block):
    wide = block.astype(jnp.float32)
    rows = []
    for at in range(0, 128, 32):
        real_part = wide[at : at + 16]
        imag_part = wide[at + 16 : at + 32]
        rows += [real_part + imag_part, imag_part - real_part]
    return jnp.concatenate(rows, axis=0).T.astype(jnp.bfloat16)


def cuts_kernel(offsets_in, records, valid, weight, cuts, table, mask, offsets, series, mask_in, in_sems):
    me = lax.axis_index("panel")
    load = pltpu.make_async_copy(offsets_in, offsets, in_sems.at[8])
    load.start()
    reads = []
    for part, (first, count) in enumerate(((0, 5248), (5248, 3968))):
        for low in range(2):
            for w in (low, low + 2):
                place = pl.ds(first, count)
                reads.append(
                    pltpu.make_async_copy(records.at[w, :, place], series[w].at[:, place], in_sems.at[part * 4 + w])
                )
    others = [
        pltpu.make_async_copy(valid, mask_in, in_sems.at[9]),
        pltpu.make_async_copy(weight, table, in_sems.at[10]),
    ]
    for copy in (*reads, *others):
        copy.start()
    load.wait()
    for part in range(2):
        for low in range(2):
            for copy in reads[part * 4 + low * 2 : part * 4 + low * 2 + 2]:
                copy.wait()

            @pl.loop(part * 8, part * 8 + 8, unroll=4)
            def _(seg):
                for half in range(2):
                    w = low + 2 * half
                    tiles = cut(series[w], offsets[me * 4 + w, seg])
                    for t in range(8):
                        cuts[low * SEG + seg, half * 64 : half * 64 + 64, t * 128 : t * 128 + 128] = tiles[t]

    for copy in others:
        copy.wait()
    for low in range(2):
        mask[low : low + 1, :] = jnp.concatenate(
            [mask_in[w : w + 1, :].astype(jnp.float32) for w in (low, low + 2)], axis=1
        )


def segments(records, valid, offsets):
    bf16 = jnp.bfloat16
    return pl.pallas_call(
        cuts_kernel,
        out_shape=(
            pltpu.VMEM((2 * SEG, 128, SEGLEN), bf16),
            pltpu.VMEM((128, SEGLEN), bf16),
            pltpu.VMEM((2, 128), jnp.float32),
        ),
        in_specs=[pl.BlockSpec(memory_space=pltpu.HBM)] * 4,
        out_specs=(pl.BlockSpec(memory_space=pltpu.VMEM),) * 3,
        scratch_shapes=[
            pltpu.SMEM((16, 16), jnp.int32),
            [pltpu.VMEM((64, 9216), bf16) for _ in range(4)],
            pltpu.VMEM((4, 64), jnp.int32),
            pltpu.SemaphoreType.DMA((11,)),
        ],
        compiler_params=pltpu.CompilerParams(vmem_limit_bytes=32 * MIB),
    )(*(pltpu.with_memory_space_constraint(a, pltpu.HBM) for a in (offsets, records, valid, weight_table(64))))


def main_kernel(
    cuts, table, mask, right, left, early, total, blocks, whole,
    own_sem, plane_send, plane_recv, ring_send, ring_recv, relay_send, relay_recv,
):
    b = lax.axis_index("bins")
    me = lax.axis_index("panel")
    x, z, core = b // 16, lax.rem(b // 2, 8), lax.rem(b, 2)
    chip = b // 2
    up, down, across = lax.rem(me + 1, 4), lax.rem(me + 3, 4), lax.rem(me + 2, 4)

    barrier = pltpu.get_barrier_semaphore()

    @pl.loop(1, 64)
    def _(i):
        pl.semaphore_signal(barrier, inc=1, device_id={"bins": lax.rem(b + i, 64)}, device_id_type=MESH)

    for there in (up, down):
        pl.semaphore_signal(barrier, inc=1, device_id={"panel": there}, device_id_type=MESH)

    def target(step, there_core):
        dx, dz = STEPS[step]
        return (lax.rem(x + dx, 4) * 8 + lax.rem(z + dz, 8)) * 2 + there_core

    for step in DIRECT:
        for there_core in range(2):
            for there in (up, down):
                place = {"bins": target(step, there_core), "panel": there}
                pl.semaphore_signal(barrier, inc=1, device_id=place, device_id_type=MESH)

    def spectra(low):
        keep = mask[low : low + 1, :]

        @pl.loop(0, SEG, unroll=4)
        def _(seg):
            spec = lax.dot_general(
                table[...], cuts[low * SEG + seg], (((1,), (1,)), ((), ())), preferred_element_type=jnp.float32
            )
            spec = spec * keep
            for part in range(2):
                total[pl.ds(part * 16 + seg, 64, stride=32), :] = spec[part * 64 : (part + 1) * 64]

        @pl.loop(0, 64, unroll=8)
        def _(k):
            blocks[k, low * 32 : low * 32 + 32] = total[pl.ds(pl.multiple_of(k * 32, 32), 32), :].astype(jnp.bfloat16)

    def send(step, first, count):
        rows = pl.ds(first, count)
        for there_core in (core, 1 - core) if step else (1 - core,):
            there = target(step, there_core)
            pltpu.make_async_remote_copy(
                blocks.at[there, rows], whole.at[me, b, rows], plane_send, plane_recv.at[chip],
                device_id={"bins": there}, device_id_type=MESH,
            ).start()

    def send_direct(first, count):
        rows = pl.ds(first, count)
        for step in DIRECT:
            for there_core in (core, 1 - core):
                there = target(step, there_core)
                for way, panel in ((0, up), (1, down)):
                    pltpu.make_async_remote_copy(
                        blocks.at[there, rows], whole.at[me, b, rows], ring_send, ring_recv.at[way, chip],
                        device_id={"bins": there, "panel": panel}, device_id_type=MESH,
                    ).start()

    spectra(0)
    pl.semaphore_wait(barrier, 65 + 4 * len(DIRECT))
    send_direct(0, 32)
    for step in range(EARLY):
        send(step, 0, 32)
    spectra(1)
    own = pltpu.make_async_copy(blocks.at[b], whole.at[me, b], own_sem)
    own.start()
    send_direct(32, 32)
    for step in range(EARLY):
        send(step, 32, 32)
    for step in range(EARLY, len(STEPS)):
        send(step, 0, 64)
    own.wait()

    def source(step):
        dx, dz = STEPS[step]
        return lax.rem(x + 4 - dx, 4) * 8 + lax.rem(z + 8 - dz, 8)

    def chunk(group, k, there, send_sem, recv_sem):
        part = whole.at[group, pl.ds(2 * k, 2)]
        return pltpu.make_async_remote_copy(
            part, part, send_sem, recv_sem, device_id={"panel": there}, device_id_type=MESH
        )

    def plane_arrival(step):
        n = 2 if step else 1
        part = blocks.at[pl.ds(0, n)]
        pltpu.make_async_remote_copy(
            part, part, plane_send, plane_recv.at[source(step)], device_id={"bins": b}, device_id_type=MESH
        ).wait_recv()

    def forward(step):
        k = source(step)
        chunk(me, k, up, ring_send, ring_recv.at[0, k]).start()
        chunk(me, k, down, ring_send, ring_recv.at[1, k]).start()

    def relay(step):
        k = source(step)
        chunk(down, k, up, ring_send, ring_recv.at[0, k]).wait_recv()
        chunk(up, k, down, ring_send, ring_recv.at[1, k]).wait_recv()
        if step % 2 == 0:
            chunk(down, k, up, relay_send, relay_recv.at[k]).start()
        else:
            chunk(up, k, down, relay_send, relay_recv.at[k]).start()

    def use(step):
        k = source(step)
        chunk(across, k, up, relay_send, relay_recv.at[k]).wait_recv()
        column = pl.ds(pl.multiple_of(k * 128, 128), 128)
        for group in range(4):
            rows = slice(group * 128, (group + 1) * 128)
            block = pair_rows(whole[group, 2 * k], whole[group, 2 * k + 1])
            right[rows, column] = block

        turned = (2 - STEPS[step][1]) % 8 * 128

        @pl.when(k // 8 == me)
        def _():
            for group in range(4):
                rows = slice(group * 128, (group + 1) * 128)
                left[turned : turned + 128, rows] = left_rows(right[rows, column])

    def multiply_early(slab):
        first = lax.rem(x + 4 - XSTEP[slab], 4) * 1024
        for half in range(2):
            wide = pl.ds(pl.multiple_of(first + half * 512, 512), 512)
            part = jnp.dot(left[:512, :], right[:, wide], preferred_element_type=jnp.float32)
            place = slab * 1024 + half * 512
            early[:, place : place + 512] = (part * SCALE).astype(jnp.bfloat16)

    last = len(STEPS)
    for step in range(last + PRODUCT_LAG):
        if step < last:
            plane_arrival(step)
            if step not in DIRECT:
                forward(step)
        if 0 <= step - RELAY_LAG < last:
            relay(step - RELAY_LAG)
        if step >= PRODUCT_LAG:
            use(step - PRODUCT_LAG)
            if 0 <= step - PRODUCT_LAG - 27 < 3:
                multiply_early(step - PRODUCT_LAG - 27)

    def sent(part, sem):
        pltpu.make_async_remote_copy(
            part, part, sem, relay_recv.at[0], device_id={"panel": up}, device_id_type=MESH
        ).wait_send()

    sent(blocks.at[pl.ds(0, 63)], plane_send)
    sent(whole.at[pl.ds(0, 2)], ring_send)
    sent(whole.at[0], relay_send)


def main(cuts, table, mask):
    dma = pltpu.SemaphoreType.DMA
    bf16 = jnp.bfloat16
    return pl.pallas_call(
        main_kernel,
        out_shape=(
            pltpu.VMEM((512, 4096), bf16),
            pltpu.VMEM((1024, 512), bf16),
            pltpu.VMEM((512, 3072), bf16),
        ),
        in_specs=[pl.BlockSpec(memory_space=pltpu.VMEM)] * 3,
        out_specs=(pl.BlockSpec(memory_space=pltpu.VMEM),) * 3,
        scratch_shapes=[
            pltpu.VMEM((64 * 32, 128), jnp.float32),
            pltpu.VMEM((64, 64, 128), bf16),
            pltpu.VMEM((4, 64, 64, 128), bf16),
            dma(()), dma(()), dma((32,)), dma(()), dma((2, 32)), dma(()), dma((32,)),
        ],
        compiler_params=pltpu.CompilerParams(
            collective_id=0, has_side_effects=True, vmem_limit_bytes=32 * MIB
        ),
        cost_estimate=pl.CostEstimate(flops=10**10, bytes_accessed=2 * 10**7, transcendentals=0),
    )(*(pltpu.with_memory_space_constraint(a, pltpu.VMEM) for a in (cuts, table, mask)))


def product_kernel(right, left, early, out, result, sems):
    b = lax.axis_index("bins")
    x, z = b // 16, lax.rem(b // 2, 8)
    copies = []

    def store(held, slab, half):
        first = pl.multiple_of(lax.rem(x + 4 - XSTEP[slab], 4) * 1024, 1024)
        for at in range(half * 4, half * 4 + 4):
            row = pl.multiple_of(lax.rem(z + 6 + at, 8) * 128, 128)
            copies.append(
                pltpu.make_async_copy(
                    held.at[pl.ds(at * 128, 128), pl.ds(slab * 1024, 1024)],
                    out.at[pl.ds(row, 128), pl.ds(first, 1024)],
                    sems.at[slab, at],
                )
            )
            copies[-1].start()

    def multiply(slab, half):
        first = lax.rem(x + 4 - XSTEP[slab], 4) * 1024
        rows = pl.ds(half * 512, 512)
        for at in range(2):
            wide = pl.ds(pl.multiple_of(first + at * 512, 512), 512)
            part = jnp.dot(left[rows, :], right[:, wide], preferred_element_type=jnp.float32)
            result[rows, pl.ds(slab * 1024 + at * 512, 512)] = (part * SCALE).astype(jnp.bfloat16)
        store(result, slab, half)

    for slab in range(3):
        store(early, slab, 0)
    multiply(3, 0)
    for slab in range(4):
        multiply(slab, 1)
    for copy in copies:
        copy.wait()


def product(right, left, early):
    return pl.pallas_call(
        product_kernel,
        out_shape=jax.ShapeDtypeStruct((1024, 4096), jnp.bfloat16),
        in_specs=[pl.BlockSpec(memory_space=pltpu.VMEM)] * 3,
        out_specs=pl.BlockSpec(memory_space=pl.ANY),
        scratch_shapes=[pltpu.VMEM((1024, 4096), jnp.bfloat16), pltpu.SemaphoreType.DMA((4, 8))],
        compiler_params=pltpu.CompilerParams(vmem_limit_bytes=32 * MIB),
    )(*(pltpu.with_memory_space_constraint(a, pltpu.VMEM) for a in (right, left, early)))


def body(records, valid, offsets):
    return product(*main(*segments(records, valid, offsets)))[None]


def solution(mesh):
    placed = (P("panel", "bins", None), P("panel", "bins"), P())
    return jax.shard_map(
        body, mesh=mesh, in_specs=placed, out_specs=P("bins", "panel", None), check_vma=False
    )
```

```python
import functools

import jax
import jax.numpy as jnp
import numpy as np
from jax import lax
from jax.experimental import pallas as pl
from jax.experimental.pallas import tpu as pltpu
from jax.sharding import PartitionSpec as P

SEGLEN = 1024
SEG = 16
BAND0 = 64
MIB = 2**20
SCALE = 1.0 / 256.0
MESH = pl.DeviceIdType.MESH


def weight_table(nbins):
    f32 = np.float32
    rows = np.arange(2 * nbins)
    freq = (BAND0 + rows % nbins)[:, None]
    pos = np.arange(SEGLEN)[None, :]
    hann = f32(0.5) - f32(0.5) * np.cos(f32(2.0 * np.pi) * pos.astype(f32) / f32(SEGLEN))
    taper = hann / np.sqrt(f32(0.375 * SEGLEN))
    phase = (freq * pos % SEGLEN).astype(f32) * f32(2.0 * np.pi / SEGLEN)
    trig = np.where((rows < nbins)[:, None], np.cos(phase), -np.sin(phase))
    return jnp.asarray((taper * trig).astype(jnp.bfloat16))


def cut(series, start):
    tile = jnp.minimum(start // 128, 63)
    inside = start - tile * 128
    base = pl.multiple_of(tile * 128, 128)
    keep = lax.broadcasted_iota(jnp.int32, (64, 128), 1) < 128 - inside
    shift = lax.rem(128 - inside, 128)
    turned = [pltpu.roll(series[:, pl.ds(base + 128 * t, 128)], shift, 1) for t in range(9)]
    return [jnp.where(keep, turned[t], turned[t + 1]) for t in range(8)]


XSTEP = (0, 1, 3, 2)
ZSTEP = (0, 1, 7, 2, 6, 3, 5, 4)
STEPS = [(dx, dz) for dx in XSTEP for dz in ZSTEP]
RELAY_LAG = 6
PRODUCT_LAG = 10
EARLY = 4
DIRECT = (8, 16, 24)


def pair_rows(even, odd):
    return jnp.concatenate(
        [
            jnp.concatenate([even[:, :64], odd[:, :64]], axis=1),
            jnp.concatenate([even[:, 64:], odd[:, 64:]], axis=1),
        ],
        axis=0,
    )


def left_rows(block):
    wide = block.astype(jnp.float32)
    rows = []
    for at in range(0, 128, 32):
        real_part = wide[at : at + 16]
        imag_part = wide[at + 16 : at + 32]
        rows += [real_part + imag_part, imag_part - real_part]
    return jnp.concatenate(rows, axis=0).T.astype(jnp.bfloat16)


def cuts_kernel(offsets_in, records, valid, weight, cuts, table, mask, offsets, series, mask_in, in_sems):
    me = lax.axis_index("panel")
    load = pltpu.make_async_copy(offsets_in, offsets, in_sems.at[8])
    load.start()
    reads = []
    for part, (first, count) in enumerate(((0, 5248), (5248, 3968))):
        for low in range(2):
            for w in (low, low + 2):
                place = pl.ds(first, count)
                reads.append(
                    pltpu.make_async_copy(records.at[w, :, place], series[w].at[:, place], in_sems.at[part * 4 + w])
                )
    others = [
        pltpu.make_async_copy(valid, mask_in, in_sems.at[9]),
        pltpu.make_async_copy(weight, table, in_sems.at[10]),
    ]
    for copy in (*reads, *others):
        copy.start()
    load.wait()
    for part in range(2):
        for low in range(2):
            for copy in reads[part * 4 + low * 2 : part * 4 + low * 2 + 2]:
                copy.wait()

            @pl.loop(part * 8, part * 8 + 8, unroll=8)
            def _(seg):
                for half in range(2):
                    w = low + 2 * half
                    tiles = cut(series[w], offsets[me * 4 + w, seg])
                    for t in range(8):
                        cuts[low * SEG + seg, half * 64 : half * 64 + 64, t * 128 : t * 128 + 128] = tiles[t]

    for copy in others:
        copy.wait()
    for low in range(2):
        mask[low : low + 1, :] = jnp.concatenate(
            [mask_in[w : w + 1, :].astype(jnp.float32) for w in (low, low + 2)], axis=1
        )


def segments(records, valid, offsets):
    bf16 = jnp.bfloat16
    return pl.pallas_call(
        cuts_kernel,
        out_shape=(
            pltpu.VMEM((2 * SEG, 128, SEGLEN), bf16),
            pltpu.VMEM((128, SEGLEN), bf16),
            pltpu.VMEM((2, 128), jnp.float32),
        ),
        in_specs=[pl.BlockSpec(memory_space=pltpu.HBM)] * 4,
        out_specs=(pl.BlockSpec(memory_space=pltpu.VMEM),) * 3,
        scratch_shapes=[
            pltpu.SMEM((16, 16), jnp.int32),
            [pltpu.VMEM((64, 9216), bf16) for _ in range(4)],
            pltpu.VMEM((4, 64), jnp.int32),
            pltpu.SemaphoreType.DMA((11,)),
        ],
        compiler_params=pltpu.CompilerParams(vmem_limit_bytes=32 * MIB),
    )(*(pltpu.with_memory_space_constraint(a, pltpu.HBM) for a in (offsets, records, valid, weight_table(64))))


def main_kernel(
    cuts, table, mask, right, left, early, total, blocks, whole,
    own_sem, plane_send, plane_recv, ring_send, ring_recv, relay_send, relay_recv,
):
    b = lax.axis_index("bins")
    me = lax.axis_index("panel")
    x, z, core = b // 16, lax.rem(b // 2, 8), lax.rem(b, 2)
    chip = b // 2
    up, down, across = lax.rem(me + 1, 4), lax.rem(me + 3, 4), lax.rem(me + 2, 4)

    barrier = pltpu.get_barrier_semaphore()

    @pl.loop(1, 64)
    def _(i):
        pl.semaphore_signal(barrier, inc=1, device_id={"bins": lax.rem(b + i, 64)}, device_id_type=MESH)

    for there in (up, down):
        pl.semaphore_signal(barrier, inc=1, device_id={"panel": there}, device_id_type=MESH)

    def target(step, there_core):
        dx, dz = STEPS[step]
        return (lax.rem(x + dx, 4) * 8 + lax.rem(z + dz, 8)) * 2 + there_core

    for step in DIRECT:
        for there_core in range(2):
            for there in (up, down):
                place = {"bins": target(step, there_core), "panel": there}
                pl.semaphore_signal(barrier, inc=1, device_id=place, device_id_type=MESH)

    def spectra(low):
        keep = mask[low : low + 1, :]

        @pl.loop(0, SEG, unroll=4)
        def _(seg):
            spec = lax.dot_general(
                table[...], cuts[low * SEG + seg], (((1,), (1,)), ((), ())), preferred_element_type=jnp.float32
            )
            spec = spec * keep
            for part in range(2):
                total[pl.ds(part * 16 + seg, 64, stride=32), :] = spec[part * 64 : (part + 1) * 64]

        @pl.loop(0, 64, unroll=8)
        def _(k):
            blocks[k, low * 32 : low * 32 + 32] = total[pl.ds(pl.multiple_of(k * 32, 32), 32), :].astype(jnp.bfloat16)

    def send(step, first, count):
        rows = pl.ds(first, count)
        for there_core in (core, 1 - core) if step else (1 - core,):
            there = target(step, there_core)
            pltpu.make_async_remote_copy(
                blocks.at[there, rows], whole.at[me, b, rows], plane_send, plane_recv.at[chip],
                device_id={"bins": there}, device_id_type=MESH,
            ).start()

    def send_direct(first, count):
        rows = pl.ds(first, count)
        for step in DIRECT:
            for there_core in (core, 1 - core):
                there = target(step, there_core)
                for way, panel in ((0, up), (1, down)):
                    pltpu.make_async_remote_copy(
                        blocks.at[there, rows], whole.at[me, b, rows], ring_send, ring_recv.at[way, chip],
                        device_id={"bins": there, "panel": panel}, device_id_type=MESH,
                    ).start()

    spectra(0)
    pl.semaphore_wait(barrier, 65 + 4 * len(DIRECT))
    send_direct(0, 32)
    for step in range(EARLY):
        send(step, 0, 32)
    spectra(1)
    own = pltpu.make_async_copy(blocks.at[b], whole.at[me, b], own_sem)
    own.start()
    send_direct(32, 32)
    for step in range(EARLY):
        send(step, 32, 32)
    for step in range(EARLY, len(STEPS)):
        send(step, 0, 64)
    own.wait()

    def source(step):
        dx, dz = STEPS[step]
        return lax.rem(x + 4 - dx, 4) * 8 + lax.rem(z + 8 - dz, 8)

    def chunk(group, k, there, send_sem, recv_sem):
        part = whole.at[group, pl.ds(2 * k, 2)]
        return pltpu.make_async_remote_copy(
            part, part, send_sem, recv_sem, device_id={"panel": there}, device_id_type=MESH
        )

    def plane_arrival(step):
        n = 2 if step else 1
        part = blocks.at[pl.ds(0, n)]
        pltpu.make_async_remote_copy(
            part, part, plane_send, plane_recv.at[source(step)], device_id={"bins": b}, device_id_type=MESH
        ).wait_recv()

    def forward(step):
        k = source(step)
        chunk(me, k, up, ring_send, ring_recv.at[0, k]).start()
        chunk(me, k, down, ring_send, ring_recv.at[1, k]).start()

    def relay(step):
        k = source(step)
        chunk(down, k, up, ring_send, ring_recv.at[0, k]).wait_recv()
        chunk(up, k, down, ring_send, ring_recv.at[1, k]).wait_recv()
        if step % 2 == 0:
            chunk(down, k, up, relay_send, relay_recv.at[k]).start()
        else:
            chunk(up, k, down, relay_send, relay_recv.at[k]).start()

    def use(step):
        k = source(step)
        chunk(across, k, up, relay_send, relay_recv.at[k]).wait_recv()
        column = pl.ds(pl.multiple_of(k * 128, 128), 128)
        for group in range(4):
            rows = slice(group * 128, (group + 1) * 128)
            block = pair_rows(whole[group, 2 * k], whole[group, 2 * k + 1])
            right[rows, column] = block

        turned = (2 - STEPS[step][1]) % 8 * 128

        @pl.when(k // 8 == me)
        def _():
            for group in range(4):
                rows = slice(group * 128, (group + 1) * 128)
                left[turned : turned + 128, rows] = left_rows(right[rows, column])

    def multiply_early(slab):
        first = lax.rem(x + 4 - XSTEP[slab], 4) * 1024
        for half in range(2):
            wide = pl.ds(pl.multiple_of(first + half * 512, 512), 512)
            part = jnp.dot(left[:512, :], right[:, wide], preferred_element_type=jnp.float32)
            place = slab * 1024 + half * 512
            early[:, place : place + 512] = (part * SCALE).astype(jnp.bfloat16)

    last = len(STEPS)
    for step in range(last + PRODUCT_LAG):
        if step < last:
            plane_arrival(step)
            if step not in DIRECT:
                forward(step)
        if 0 <= step - RELAY_LAG < last:
            relay(step - RELAY_LAG)
        if step >= PRODUCT_LAG:
            use(step - PRODUCT_LAG)
            if 0 <= step - PRODUCT_LAG - 27 < 3:
                multiply_early(step - PRODUCT_LAG - 27)

    def sent(part, sem):
        pltpu.make_async_remote_copy(
            part, part, sem, relay_recv.at[0], device_id={"panel": up}, device_id_type=MESH
        ).wait_send()

    sent(blocks.at[pl.ds(0, 63)], plane_send)
    sent(whole.at[pl.ds(0, 2)], ring_send)
    sent(whole.at[0], relay_send)


def main(cuts, table, mask):
    dma = pltpu.SemaphoreType.DMA
    bf16 = jnp.bfloat16
    return pl.pallas_call(
        main_kernel,
        out_shape=(
            pltpu.VMEM((512, 4096), bf16),
            pltpu.VMEM((1024, 512), bf16),
            pltpu.VMEM((512, 3072), bf16),
        ),
        in_specs=[pl.BlockSpec(memory_space=pltpu.VMEM)] * 3,
        out_specs=(pl.BlockSpec(memory_space=pltpu.VMEM),) * 3,
        scratch_shapes=[
            pltpu.VMEM((64 * 32, 128), jnp.float32),
            pltpu.VMEM((64, 64, 128), bf16),
            pltpu.VMEM((4, 64, 64, 128), bf16),
            dma(()), dma(()), dma((32,)), dma(()), dma((2, 32)), dma(()), dma((32,)),
        ],
        compiler_params=pltpu.CompilerParams(
            collective_id=0, has_side_effects=True, vmem_limit_bytes=32 * MIB
        ),
        cost_estimate=pl.CostEstimate(flops=10**10, bytes_accessed=2 * 10**7, transcendentals=0),
    )(*(pltpu.with_memory_space_constraint(a, pltpu.VMEM) for a in (cuts, table, mask)))


def product_kernel(right, left, early, out, result, sems):
    b = lax.axis_index("bins")
    x, z = b // 16, lax.rem(b // 2, 8)
    copies = []

    def store(held, slab, half):
        first = pl.multiple_of(lax.rem(x + 4 - XSTEP[slab], 4) * 1024, 1024)
        for at in range(half * 4, half * 4 + 4):
            row = pl.multiple_of(lax.rem(z + 6 + at, 8) * 128, 128)
            copies.append(
                pltpu.make_async_copy(
                    held.at[pl.ds(at * 128, 128), pl.ds(slab * 1024, 1024)],
                    out.at[pl.ds(row, 128), pl.ds(first, 1024)],
                    sems.at[slab, at],
                )
            )
            copies[-1].start()

    def multiply(slab, half):
        first = lax.rem(x + 4 - XSTEP[slab], 4) * 1024
        rows = pl.ds(half * 512, 512)
        for at in range(2):
            wide = pl.ds(pl.multiple_of(first + at * 512, 512), 512)
            part = jnp.dot(left[rows, :], right[:, wide], preferred_element_type=jnp.float32)
            result[rows, pl.ds(slab * 1024 + at * 512, 512)] = (part * SCALE).astype(jnp.bfloat16)
        store(result, slab, half)

    for slab in range(3):
        store(early, slab, 0)
    multiply(3, 0)
    for slab in range(4):
        multiply(slab, 1)
    for copy in copies:
        copy.wait()


def product(right, left, early):
    return pl.pallas_call(
        product_kernel,
        out_shape=jax.ShapeDtypeStruct((1024, 4096), jnp.bfloat16),
        in_specs=[pl.BlockSpec(memory_space=pltpu.VMEM)] * 3,
        out_specs=pl.BlockSpec(memory_space=pl.ANY),
        scratch_shapes=[pltpu.VMEM((1024, 4096), jnp.bfloat16), pltpu.SemaphoreType.DMA((4, 8))],
        compiler_params=pltpu.CompilerParams(vmem_limit_bytes=32 * MIB),
    )(*(pltpu.with_memory_space_constraint(a, pltpu.VMEM) for a in (right, left, early)))


def body(records, valid, offsets):
    return product(*main(*segments(records, valid, offsets)))[None]


def solution(mesh):
    placed = (P("panel", "bins", None), P("panel", "bins"), P())
    return jax.shard_map(
        body, mesh=mesh, in_specs=placed, out_specs=P("bins", "panel", None), check_vma=False
    )
```
